32 devices in a mesh: grp: 2 (over y), row: 4 (over x, core), col: 4 (over z).
Axes of the slice: x: 2, y: 2, z: 4, core: 2. Of those that a mesh axis runs over, the one named last changes fastest.
Arguments:
- factor: float32 [8, 4, 768, 768], P(('grp', 'row'), 'col'), parts along dimension 0
- rhs: float32 [8, 768, 64], P(('grp', 'row')), parts along dimension 0, may hold values from -6 to 6
- pattern: int32 [8, 4], P('grp'), parts along dimension 0, may hold values from 0 to 1, as said below
Outputs:
- solution: float32 [8, 768, 64], P(('grp', 'col'), 'row'), parts along dimension 0
The draws below stay inside these ranges and needn't reach their ends.
There are 2 independent parts, one for each index of `grp`. The reference program is written for one: setup_inputs(seed, part) draws one part's arguments, and reference() takes and returns one part's arrays. A program takes and returns all parts, laid end to end along the dimension named above; each array names one. Nothing has to cross between parts.
Inputs may be any that keep to these rules, and one draw needn't show every extreme that they name: pattern[i, j] = 1 only where j < i; the blocks form an elimination tree in which every block but the last has exactly one parent p > j with pattern[p, j] = 1, and pattern[i, j] = 1 only where i is an ancestor of j; every chain of blocks linked by pattern has at most 4 blocks and some chain has exactly 4.
All inputs are finite; a program needn't handle non-finite values.
Results may differ from the reference program's by a relative error of at most 0.0001.
Values sent between devices are 32-bit elements; how exact they have to be, the bound alone decides.
No kernel may reach another device: no remote copies, remote signals or barrier semaphores. Data moves between devices by JAX's collectives and lax.ppermute only.
A program may use at most 64 MiB of HBM per device.

```python
import jax
import jax.numpy as jnp
from jax import lax

TILE = 768
RHS = 64
BLOCKS = 4
LEVELS = 4


def draw_factor(key, part):
    key_base, key_diag = jax.random.split(jax.random.fold_in(key, 11))
    shape_all = (BLOCKS, BLOCKS, TILE, TILE)
    base = jax.random.normal(key_base, shape_all, jnp.float32)
    diag_values = jnp.exp(jax.random.uniform(key_diag, (BLOCKS, 1, TILE, 1), jnp.float32, jnp.log(0.5), jnp.log(2.0)))
    identity = jnp.eye(TILE, dtype=jnp.float32)
    on_diagonal = (jnp.arange(BLOCKS)[:, None] == jnp.arange(BLOCKS)[None, :])[:, :, None, None]
    dominant = base * (0.5 / jnp.sqrt(TILE * 1.0)) + diag_values * identity
    return jnp.where(on_diagonal, dominant, base / jnp.sqrt(8.0 * TILE))


def draw_pattern(key, part):
    key_parent, key_bits = jax.random.split(jax.random.fold_in(key, 7))
    indices = jnp.arange(BLOCKS, dtype=jnp.int32)
    spine_start = BLOCKS - LEVELS
    leaf_parent = spine_start + jax.random.randint(key_parent, (BLOCKS,), 1, LEVELS, dtype=jnp.int32)
    parents = jnp.where(indices >= spine_start, indices + 1, leaf_parent)
    position = jnp.where(indices >= spine_start, indices - spine_start, leaf_parent - spine_start - 1)
    ancestor = (indices[:, None] >= spine_start) & (indices[:, None] - spine_start > position[None, :])
    random_bits = jax.random.randint(key_bits, (BLOCKS, BLOCKS), 0, 2, dtype=jnp.int32)
    is_parent = indices[:, None] == parents[None, :]
    return jnp.where(ancestor, jnp.where(is_parent, 1, random_bits), 0).astype(jnp.int32)


def steps_of(own_key, shape, pieces, smallest, high):
    loudness = 1.0
    for axis_at, parts in pieces:
        draws = jax.random.uniform(jax.random.fold_in(jax.random.fold_in(own_key, 6), axis_at), (parts,), jnp.float32, smallest / len(pieces), high / len(pieces))
        loudness = loudness * jnp.repeat(jnp.exp(draws), shape[axis_at] // parts).reshape((-1,) + (1,) * (len(shape) - 1 - axis_at))
    return loudness


def normal_values(stream_key, shape, deviation, reach, cuts=(), kind=jnp.bfloat16):
    level = steps_of(stream_key, shape, cuts, -0.22, 0.18) if cuts else 1.0
    entries = jax.random.normal(stream_key, shape, jnp.float32) * deviation * level
    return jnp.minimum(jnp.maximum(entries, -reach), reach).astype(kind)


def setup_inputs(seed: int = 0, part: int = 0) -> dict:
    key_list = jax.random.split(jax.random.key(seed), 4)
    part_keys = jax.random.split(jax.random.fold_in(key_list[3], part), 4)
    return {
        "factor": draw_factor(jax.random.fold_in(jax.random.fold_in(key_list[3], part), 71), part),
        "rhs": normal_values(part_keys[1], (BLOCKS, TILE, RHS), 1.0, 6.0, ((0, 4),), jnp.float32),
        "pattern": draw_pattern(jax.random.fold_in(jax.random.fold_in(key_list[3], part), 71), part),
    }


def reference(factor, rhs, pattern):
    solved = jnp.zeros((BLOCKS, TILE, RHS), jnp.float32)
    for block_index in range(BLOCKS):
        weights = (pattern[block_index] == 1).astype(jnp.float32)
        carried = jnp.einsum("jab,jbr->ar", factor[block_index], solved * weights[:, None, None], precision=lax.Precision.HIGHEST)
        answer = jnp.dot(factor[block_index, block_index], rhs[block_index] - carried, precision=lax.Precision.HIGHEST, preferred_element_type=jnp.float32)
        solved = solved.at[block_index].set(answer)
    return solved
```

```python
import functools

import jax
import jax.numpy as jnp
from jax import lax
from jax.experimental import pallas as pl
from jax.experimental.pallas import tpu as pltpu
from jax.sharding import PartitionSpec as P

GRID = ("row", "col")
PIECES = 1
LOADS = 6
FLAT = (((1,), (0,)), ((), ()))
TURNED = (((1,), (1,)), ((), ()))
SIDE = 4


def split(values):
    big = values.astype(jnp.bfloat16)
    return big, (values - big.astype(jnp.float32)).astype(jnp.bfloat16)


def product(columns, big, small, dims):
    count = columns.shape[0]
    high, low = split(columns)
    dot = functools.partial(lax.dot_general, dimension_numbers=dims, preferred_element_type=jnp.float32)
    both = dot(jnp.concatenate([high, low], 0), big)
    return both[:count] + (both[count:] + dot(high, small))


def here(row, col):
    return (lax.axis_index("row") == row) & (lax.axis_index("col") == col)


def call(kernel, name, outs, args, spaces=None, scratch=(), flops=0, size=0):
    spaces = spaces or [pltpu.VMEM] * len(args)
    return pl.pallas_call(
        kernel,
        out_shape=outs,
        in_specs=[pl.BlockSpec(memory_space=space) for space in spaces],
        out_specs=jax.tree.map(lambda _: pl.BlockSpec(memory_space=pltpu.VMEM), outs),
        scratch_shapes=scratch,
        compiler_params=pltpu.CompilerParams(vmem_limit_bytes=24 << 20),
        cost_estimate=pl.CostEstimate(flops=flops, bytes_accessed=size, transcendentals=0),
        name=name,
    )(*args)


def like(array, dtype=None, shape=None):
    return jax.ShapeDtypeStruct(shape or array.shape, dtype or array.dtype)


def load_block(factor_hbm, right, pattern, big_ref, small_ref, *rest):
    found, (buffer, sems) = rest[:-2], rest[-2:]
    order = right.shape[1]
    rows = order // LOADS
    copies = [
        pltpu.make_async_copy(factor_hbm.at[pl.ds(k * rows, rows)], buffer.at[pl.ds(k * rows, rows)], sems.at[k])
        for k in range(LOADS)
    ]
    for copy in copies:
        copy.start()
    row, col = lax.axis_index("row"), lax.axis_index("col")
    first = here(0, 0)
    used = (row == col) | (pattern[row, col] == 1)
    for k, copy in enumerate(copies):
        copy.wait()
        part = slice(k * rows, (k + 1) * rows)

        @pl.when(first)
        def _():
            answer = product(right[...], *split(buffer[part]), TURNED)
            count = found[0].shape[0]
            for n, ref in enumerate(found):
                ref[:, part] = answer[n * count : (n + 1) * count]

        @pl.when(jnp.logical_not(first))
        def _():
            block = jnp.where(used, buffer[part], 0.0).T
            big_ref[:, part], small_ref[:, part] = split(block)

    @pl.when(jnp.logical_not(first))
    def _():
        for ref in found:
            ref[...] = jnp.zeros_like(ref)


def load_below(factor, pattern, big_ref, small_ref):
    @pl.when(here(2, 2))
    def _():
        block = jnp.where(pattern[3, 2] == 1, factor[...], 0.0).T
        big_ref[...], small_ref[...] = split(block)


def step_first(big, small, held, got, out):
    out[...] = held[...]

    @pl.when(here(1, 0))
    def _():
        out[...] = product(got[...], big[...], small[...], FLAT)


def step_second(big, small, held, right, early, got, out):
    out[...] = held[...]

    def put(columns):
        out[...] = product(columns, big[...], small[...], FLAT)

    @pl.when(here(1, 1))
    def _():
        put(right[...] - got[...])

    @pl.when(here(2, 0))
    def _():
        put(early[...])

    @pl.when(here(3, 0))
    def _():
        put(got[...])


def step_third(big, small, held, got, out):
    out[...] = held[...]

    @pl.when(here(2, 1))
    def _():
        out[...] = product(got[...], big[...], small[...], FLAT)


def step_beside(big, small, held, got, out):
    out[...] = held[...]

    @pl.when(here(3, 1))
    def _():
        out[...] = product(got[...], big[...], small[...], FLAT)


def step_fourth(big, small, below_big, below_small, held, right, early, got, out, carried):
    out[...] = held[...]
    carried[...] = jnp.zeros_like(carried)

    @pl.when(here(2, 2))
    def _():
        answer = product(right[...] - early[...] - got[...], big[...], small[...], FLAT)
        out[...] = answer
        carried[...] = product(answer, below_big[...], below_small[...], FLAT)


def step_last(big, small, held, right, early, middle, got, out, *shares):
    out[...] = held[...]

    @pl.when(here(3, 3))
    def _():
        columns = right[...] - early[...] - middle[...] - got[...]
        out[...] = product(columns, big[...], small[...], FLAT)

    wide = out.shape[1] // SIDE
    row = lax.axis_index("row")
    for k in range(SIDE):

        @pl.when(row == (k ^ 1))
        def _():
            shares[0][...] = out[:, k * wide : (k + 1) * wide]

    for k in range(2):
        shares[k + 1][...] = out[:, k * wide : (k + 1) * wide]


def give(held, first, early, second, third, beside, across, zero, one, out):
    wide = out.shape[1]
    whole = {
        (0, 0): held, (1, 0): first, (2, 0): early, (3, 0): second,
        (1, 1): held, (2, 1): third, (3, 1): beside,
        (2, 2): held, (3, 3): held,
    }
    share = {(0, 1): across, (3, 2): across, (2, 3): across, (0, 2): zero, (0, 3): zero, (1, 2): one, (1, 3): one}
    for (row, col), ref in whole.items():

        @pl.when(here(row, col))
        def _(row=row, ref=ref):
            out[...] = ref[:, row * wide : (row + 1) * wide]

    for (row, col), ref in share.items():

        @pl.when(here(row, col))
        def _(ref=ref):
            out[...] = ref[...]


def route(*cycles):
    target = {}
    for cycle in cycles:
        for spot, source in enumerate(cycle):
            target[source] = cycle[(spot + 1) % len(cycle)]
    for row in range(SIDE):
        for col in range(SIDE):
            target.setdefault((row, col), (row ^ 1, col))
    assert sorted(target) == sorted(target.values())
    return [(a * SIDE + b, c * SIDE + d) for (a, b), (c, d) in target.items()]


SWAP = route()
EARLY = route([(0, 0), (2, 0), (3, 0), (1, 0)])
SECOND = route([(1, 0), (1, 1), (0, 1), (0, 0), (3, 0), (2, 0)])
THIRD = route([(1, 1), (2, 1), (0, 1)], [(2, 0), (2, 2), (3, 2), (3, 0), (2, 3), (3, 3), (3, 1)])
FOURTH = route([(2, 1), (2, 2)], [(3, 1), (3, 3), (2, 3), (3, 2)])
LAST = route([(2, 2), (3, 3), (2, 3), (3, 2)])
TO_ZERO = route([(3, 3), (0, 3), (1, 3), (2, 3)], [(2, 2), (0, 2), (1, 2), (3, 2)])
TO_ONE = route([(3, 3), (1, 3), (0, 3), (2, 3)], [(2, 2), (1, 2), (0, 2), (3, 2)])
BELOW = [(3 * SIDE + 2, 2 * SIDE + 2)]


def send(pairs, arrays):
    return [lax.ppermute(array, GRID, pairs) for array in arrays]


def chain(factor, rhs, pattern):
    block = factor[0, 0]
    order = block.shape[0]
    right = rhs[0].T
    count = right.shape[0] // PIECES
    pieces = [right[k * count : (k + 1) * count] for k in range(PIECES)]
    half = like(block, jnp.bfloat16)
    vector = like(pieces[0])
    work = 6 * order * order * count

    def each(kernel, name, outs, *lists, shared=()):
        return [
            call(kernel, name, outs, (*shared, *args), flops=work, size=4 * order * order) for args in zip(*lists)
        ]

    big, small, *held = call(
        load_block, "load_block", [half, half] + [vector] * PIECES, (block, right, pattern),
        [pltpu.HBM, pltpu.VMEM, pltpu.SMEM],
        [pltpu.VMEM(block.shape, block.dtype), pltpu.SemaphoreType.DMA((LOADS,))],
        6 * work, 8 * order * order,
    )
    shared = (big, small)
    first = send(SWAP, held)
    (below,) = send(BELOW, [block])
    early = send(EARLY, held)
    held = each(step_first, "step_first", vector, held, first, shared=shared)
    second = send(SECOND, held)
    held = each(step_second, "step_second", vector, held, pieces, early, second, shared=shared)
    third = send(THIRD, held)
    beside = send(SWAP, third)
    held = each(step_third, "step_third", vector, held, third, shared=shared)
    held = each(step_beside, "step_beside", vector, held, beside, shared=shared)
    fourth = send(FOURTH, held)
    under = call(
        load_below, "load_below", [half, half], (below, pattern), [pltpu.VMEM, pltpu.SMEM], flops=work, size=8 * order * order
    )
    pairs = each(step_fourth, "step_fourth", [vector, vector], held, pieces, third, fourth, shared=(*shared, *under))
    held = [pair[0] for pair in pairs]
    last = send(LAST, [pair[1] for pair in pairs])
    share = like(pieces[0], shape=(count, order // SIDE))
    ends = each(step_last, "step_last", [vector] + [share] * 3, held, pieces, beside, fourth, last, shared=shared)
    held = [end[0] for end in ends]
    across = send(SWAP, [end[1] for end in ends])
    zero = send(TO_ZERO, [end[2] for end in ends])
    one = send(TO_ONE, [end[3] for end in ends])
    given = each(give, "give", share, held, first, early, second, third, beside, across, zero, one)
    return jnp.concatenate(given, 0).T[None]


def from_root(shard, axis, root):
    mine = lax.axis_index(axis) == root
    return lax.psum(jnp.where(mine, shard, jnp.zeros_like(shard)), axis)


def multiply(factor_tile, columns):
    return jnp.dot(factor_tile, columns, precision=lax.Precision.HIGHEST, preferred_element_type=jnp.float32)


def levels(factor, rhs, pattern):
    block, right = factor[0, 0], rhs[0]
    row, col = lax.axis_index("row"), lax.axis_index("col")
    depth = min(6, lax.axis_size("row"))
    height = jnp.zeros((pattern.shape[0],), jnp.int32)
    for _ in range(depth):
        height = jnp.max(jnp.where(pattern == 1, height[None, :] + 1, 0), axis=1)
    solved = carried = jnp.zeros_like(right)
    times = functools.partial(multiply, block)
    for level in range(depth):
        solve_now = (row == col) & (height[row] == level)
        fresh = lax.cond(solve_now, times, jnp.zeros_like, right - carried)
        arrived = from_root(fresh, "row", col)
        if level < depth - 1:
            apply_now = (pattern[row, col] == 1) & (height[col] == level)
            carried = carried + lax.psum(lax.cond(apply_now, times, jnp.zeros_like, arrived), "col")
        solved = solved + arrived
    share = solved.shape[0] // lax.axis_size("row")
    return lax.dynamic_slice_in_dim(solved, row * share, share, 0)[None]


def solution(mesh):
    in_specs = (P(("grp", "row"), "col", None, None), P(("grp", "row"), None, None), P("grp", None))
    out_specs = P(("grp", "col"), "row", None)
    local = chain if mesh.shape["row"] == mesh.shape["col"] == SIDE else levels
    return jax.shard_map(local, mesh=mesh, in_specs=in_specs, out_specs=out_specs, check_vma=False)
```

```python
import functools

import jax
import jax.numpy as jnp
from jax import lax
from jax.experimental import pallas as pl
from jax.experimental.pallas import tpu as pltpu
from jax.sharding import PartitionSpec as P

GRID = ("row", "col")
LOADS = 3
FLAT = (((1,), (0,)), ((), ()))
TURNED = (((1,), (1,)), ((), ()))
SIDE = 4


def split(values):
    big = values.astype(jnp.bfloat16)
    return big, (values - big.astype(jnp.float32)).astype(jnp.bfloat16)


def product(columns, big, small, dims):
    count = columns.shape[0]
    high, low = split(columns)
    dot = functools.partial(lax.dot_general, dimension_numbers=dims, preferred_element_type=jnp.float32)
    both = dot(jnp.concatenate([high, low], 0), big)
    return both[:count] + (both[count:] + dot(high, small))


def here(row, col):
    return (lax.axis_index("row") == row) & (lax.axis_index("col") == col)


def call(kernel, name, outs, args, spaces=None, scratch=(), flops=0, size=0):
    spaces = spaces or [pltpu.VMEM] * len(args)
    many = isinstance(outs, list)
    kept = [pltpu.VMEM(out.shape, out.dtype) for out in (outs if many else [outs])]
    args = [pltpu.with_memory_space_constraint(a, s) if s is pltpu.HBM else a for a, s in zip(args, spaces)]
    found = pl.pallas_call(
        kernel,
        out_shape=kept,
        in_specs=[pl.BlockSpec(memory_space=space) for space in spaces],
        out_specs=[pl.BlockSpec(memory_space=pltpu.VMEM)] * len(kept),
        scratch_shapes=scratch,
        compiler_params=pltpu.CompilerParams(vmem_limit_bytes=24 << 20),
        cost_estimate=pl.CostEstimate(flops=flops, bytes_accessed=size, transcendentals=0),
        name=name,
    )(*args)
    return found if many else found[0]


def like(array, dtype=None, shape=None):
    return jax.ShapeDtypeStruct(shape or array.shape, dtype or array.dtype)


def fetch(factor_hbm, pattern_hbm, buffer, links, sems):
    rows = buffer.shape[0] // LOADS
    copies = [pltpu.make_async_copy(pattern_hbm, links, sems.at[LOADS])]
    for k in range(LOADS):
        part = pl.ds(k * rows, rows)
        copies.append(pltpu.make_async_copy(factor_hbm.at[part], buffer.at[part], sems.at[k]))
    for copy in copies:
        copy.start()
    return copies


def turn_block(copies, buffer, links, big_ref, small_ref):
    row, col = lax.axis_index("row"), lax.axis_index("col")
    copies[0].wait()
    used = (row == col) | (links[row, col] == 1)
    rows = buffer.shape[0] // LOADS
    for k in range(LOADS):
        copies[k + 1].wait()
        part = slice(k * rows, (k + 1) * rows)
        big_ref[:, part], small_ref[:, part] = split(jnp.where(used, buffer[part], 0.0).T)


def open_chain(factor_hbm, right_hbm, pattern_hbm, right, big_ref, small_ref, found, buffer, links, sems):
    load = pltpu.make_async_copy(right_hbm, right, sems.at[LOADS + 1])
    load.start()

    @pl.when(here(0, 0))
    def _():
        copies = fetch(factor_hbm, pattern_hbm, buffer, links, sems)
        load.wait()
        rows = buffer.shape[0] // LOADS
        for k in range(LOADS):
            copies[k + 1].wait()
            part = slice(k * rows, (k + 1) * rows)
            found[:, part] = product(right[...], *split(buffer[part]), TURNED)
        copies[0].wait()

    @pl.when(here(1, 0))
    def _():
        turn_block(fetch(factor_hbm, pattern_hbm, buffer, links, sems), buffer, links, big_ref, small_ref)

    @pl.when(jnp.logical_not(here(0, 0)))
    def _():
        load.wait()
        found[...] = jnp.zeros_like(found)


def load_block(factor_hbm, pattern_hbm, after, big_ref, small_ref, buffer, links, sems):
    row, col = lax.axis_index("row"), lax.axis_index("col")

    @pl.when((row >= col) & jnp.logical_not(here(0, 0) | here(1, 0)))
    def _():
        turn_block(fetch(factor_hbm, pattern_hbm, buffer, links, sems), buffer, links, big_ref, small_ref)


def advance(rules, plain, big, small, held, *refs):
    sources, out = refs[:-1], refs[-1]
    out[...] = held[...]
    for spot in sorted({*rules, *plain}):

        @pl.when(here(*spot))
        def _(spot=spot):
            given = [source[...] for source in sources]
            terms = [product(rules[spot](*given), big[...], small[...], FLAT)] if spot in rules else []
            terms += [plain[spot](*given)] if spot in plain else []
            out[...] = sum(terms[1:], terms[0])


def share_of(ref, row):
    wide = ref.shape[1] // SIDE
    return ref[:, row * wide : (row + 1) * wide]


def step_two(big, small, held, third, out, aside):
    out[...] = held[...]
    aside[...] = held[...]

    @pl.when(here(2, 1) | here(3, 0))
    def _():
        out[...] = product(third[...], big[...], small[...], FLAT)

    @pl.when(here(2, 1))
    def _():
        aside[...] = third[...]


def pass_two(big, small, held, right, early, got, out, zero, one):
    out[...] = held[...]

    @pl.when(here(2, 2))
    def _():
        out[...] = product(right[...] - early[...] - got[...], big[...], small[...], FLAT)

    zero[...] = share_of(out, 0)
    one[...] = share_of(out, 1)


def close_chain(big, small, held, right, middle, got, out, across, zero, one):
    out[...] = held[...]

    @pl.when(here(3, 3))
    def _():
        columns = right[...] - middle[...] - got[...]
        out[...] = product(columns, big[...], small[...], FLAT)

    row = lax.axis_index("row")
    for k in range(SIDE):

        @pl.when(row == (k ^ 1))
        def _():
            across[...] = share_of(out, k)

    zero[...] = share_of(out, 0)
    one[...] = share_of(out, 1)


def give(held, first, second, third, beside, inside, across, zero_two, one_two, zero, one, out):
    whole = {
        (0, 0): held, (1, 0): first, (2, 0): second, (3, 0): third,
        (1, 1): held, (2, 1): third, (3, 1): beside,
        (2, 2): held, (3, 2): inside, (3, 3): held,
    }
    share = {
        (0, 1): across, (2, 3): across,
        (0, 2): zero_two, (1, 2): one_two, (0, 3): zero, (1, 3): one,
    }
    for (row, col), ref in whole.items():

        @pl.when(here(row, col))
        def _(row=row, ref=ref):
            out[...] = share_of(ref, row)

    for (row, col), ref in share.items():

        @pl.when(here(row, col))
        def _(ref=ref):
            out[...] = ref[...]


def route(*cycles):
    target = {}
    for cycle in cycles:
        for spot, source in enumerate(cycle):
            target[source] = cycle[(spot + 1) % len(cycle)]
    for row in range(SIDE):
        for col in range(SIDE):
            target.setdefault((row, col), (row ^ 1, col))
    assert sorted(target) == sorted(target.values())
    return [(a * SIDE + b, c * SIDE + d) for (a, b), (c, d) in target.items()]


SWAP = route()
TO_11 = route([(1, 0), (1, 1), (0, 1), (0, 0), (2, 0), (3, 0)])
TO_21 = route([(1, 1), (2, 1), (0, 1)], [(0, 0), (3, 0), (2, 0), (3, 1), (1, 0)])
TO_22 = route([(2, 1), (2, 2), (3, 2), (2, 0), (3, 0), (3, 1)])
BESIDE = route([(2, 1), (3, 1)], [(2, 0), (2, 2), (3, 2), (1, 2), (0, 2), (3, 0)])
MIDDLE = route([(3, 1), (3, 3), (2, 3), (2, 1)])
TO_33 = route([(3, 2), (3, 3), (2, 3), (2, 2)])
TO_02 = route([(2, 2), (0, 2)], [(3, 2), (1, 2)])
TO_12 = route([(2, 2), (1, 2)], [(3, 2), (0, 2)])
TO_03 = route([(3, 3), (0, 3), (1, 3), (2, 3)])
TO_13 = route([(3, 3), (1, 3), (0, 3), (2, 3)])


def send(pairs, array):
    return lax.ppermute(array, GRID, pairs)


def chain(factor, rhs, pattern):
    block = factor[0, 0]
    order = block.shape[0]
    turned = rhs[0].T
    half, vector = like(block, jnp.bfloat16), like(turned)
    work = 6 * order * order * turned.shape[0]
    weight = dict(flops=work, size=4 * order * order)
    buffers = [pltpu.VMEM(block.shape, block.dtype), pltpu.SMEM(pattern.shape, pattern.dtype)]

    def move(name, rules, held, *sources, shared, plain={}):
        return call(functools.partial(advance, rules, plain), name, vector, (*shared, held, *sources), **weight)

    right, big, small, held = call(
        open_chain, "open_chain", [vector, half, half, vector], (block, turned, pattern), [pltpu.HBM] * 3,
        buffers + [pltpu.SemaphoreType.DMA((LOADS + 2,))], **weight,
    )
    first = send(SWAP, held)
    carried = move("product_10", {(1, 0): lambda first: first}, held, first, shared=(big, small))
    second = send(TO_11, carried)
    shared = call(
        load_block, "load_block", [half, half], (block, pattern, carried), [pltpu.HBM, pltpu.HBM, pltpu.VMEM],
        buffers + [pltpu.SemaphoreType.DMA((LOADS + 1,))], **weight,
    )
    rules = {(1, 1): lambda right, second: right - second, (2, 0): lambda right, second: second}
    held = move("solve_1", rules, held, right, second, shared=shared)
    third = send(TO_21, held)
    carried, aside = call(step_two, "product_21", [vector, vector], (*shared, held, third), **weight)
    fourth, beside = send(TO_22, carried), send(BESIDE, aside)
    middle = move(
        "product_31", {(3, 1): lambda beside, fourth: beside}, carried, beside, fourth, shared=shared,
        plain={(3, 1): lambda beside, fourth: fourth},
    )
    middle = send(MIDDLE, middle)
    share = like(turned, shape=(turned.shape[0], order // SIDE))
    held, zero_two, one_two = call(
        pass_two, "solve_2", [vector, share, share], (*shared, held, right, beside, fourth), **weight
    )
    inside = send(SWAP, held)
    carried = move("product_32", {(3, 2): lambda got: got}, carried, inside, shared=shared)
    last = send(TO_33, carried)
    zero_two, one_two = send(TO_02, zero_two), send(TO_12, one_two)
    held, across, zero, one = call(
        close_chain, "solve_3", [vector] + [share] * 3, (*shared, held, right, middle, last), **weight
    )
    across, zero, one = send(SWAP, across), send(TO_03, zero), send(TO_13, one)
    given = call(give, "give", share, (held, first, second, third, beside, inside, across, zero_two, one_two, zero, one))
    return given.T[None]


def from_root(shard, axis, root):
    mine = lax.axis_index(axis) == root
    return lax.psum(jnp.where(mine, shard, jnp.zeros_like(shard)), axis)


def multiply(factor_tile, columns):
    return jnp.dot(factor_tile, columns, precision=lax.Precision.HIGHEST, preferred_element_type=jnp.float32)


def levels(factor, rhs, pattern):
    block, right = factor[0, 0], rhs[0]
    row, col = lax.axis_index("row"), lax.axis_index("col")
    depth = min(6, lax.axis_size("row"))
    height = jnp.zeros((pattern.shape[0],), jnp.int32)
    for _ in range(depth):
        height = jnp.max(jnp.where(pattern == 1, height[None, :] + 1, 0), axis=1)
    solved = carried = jnp.zeros_like(right)
    times = functools.partial(multiply, block)
    for level in range(depth):
        solve_now = (row == col) & (height[row] == level)
        fresh = lax.cond(solve_now, times, jnp.zeros_like, right - carried)
        arrived = from_root(fresh, "row", col)
        if level < depth - 1:
            apply_now = (pattern[row, col] == 1) & (height[col] == level)
            carried = carried + lax.psum(lax.cond(apply_now, times, jnp.zeros_like, arrived), "col")
        solved = solved + arrived
    share = solved.shape[0] // lax.axis_size("row")
    return lax.dynamic_slice_in_dim(solved, row * share, share, 0)[None]


def solution(mesh):
    in_specs = (P(("grp", "row"), "col", None, None), P(("grp", "row"), None, None), P("grp", None))
    out_specs = P(("grp", "col"), "row", None)
    local = chain if mesh.shape["row"] == mesh.shape["col"] == SIDE else levels
    return jax.shard_map(local, mesh=mesh, in_specs=in_specs, out_specs=out_specs, check_vma=False)
```

```python
import functools

import jax
import jax.numpy as jnp
from jax import lax
from jax.experimental import pallas as pl
from jax.experimental.pallas import tpu as pltpu
from jax.sharding import PartitionSpec as P

GRID = ("row", "col")
LOADS = 3
PIECES = 2
FLAT = (((1,), (0,)), ((), ()))
TURNED = (((1,), (1,)), ((), ()))
SIDE = 4


def split(values):
    big = values.astype(jnp.bfloat16)
    return big, (values - big.astype(jnp.float32)).astype(jnp.bfloat16)


def product(columns, big, small, dims):
    count = columns.shape[0]
    high, low = split(columns)
    dot = functools.partial(lax.dot_general, dimension_numbers=dims, preferred_element_type=jnp.float32)
    both = dot(jnp.concatenate([high, low], 0), big)
    return both[:count] + (both[count:] + dot(high, small))


def here(row, col):
    return (lax.axis_index("row") == row) & (lax.axis_index("col") == col)


def call(kernel, name, outs, args, spaces=None, scratch=(), flops=0, size=0):
    spaces = spaces or [pltpu.VMEM] * len(args)
    many = isinstance(outs, list)
    kept = [pltpu.VMEM(out.shape, out.dtype) for out in (outs if many else [outs])]
    args = [pltpu.with_memory_space_constraint(a, s) if s is pltpu.HBM else a for a, s in zip(args, spaces)]
    found = pl.pallas_call(
        kernel,
        out_shape=kept,
        in_specs=[pl.BlockSpec(memory_space=space) for space in spaces],
        out_specs=[pl.BlockSpec(memory_space=pltpu.VMEM)] * len(kept),
        scratch_shapes=scratch,
        compiler_params=pltpu.CompilerParams(vmem_limit_bytes=24 << 20),
        cost_estimate=pl.CostEstimate(flops=flops, bytes_accessed=size, transcendentals=0),
        name=name,
    )(*args)
    return found if many else found[0]


def like(array, dtype=None, shape=None):
    return jax.ShapeDtypeStruct(shape or array.shape, dtype or array.dtype)


def fetch(factor_hbm, pattern_hbm, buffer, links, sems):
    rows = buffer.shape[0] // LOADS
    copies = [pltpu.make_async_copy(pattern_hbm, links, sems.at[LOADS])]
    for k in range(LOADS):
        part = pl.ds(k * rows, rows)
        copies.append(pltpu.make_async_copy(factor_hbm.at[part], buffer.at[part], sems.at[k]))
    for copy in copies:
        copy.start()
    return copies


def turn_block(copies, buffer, links, big_ref, small_ref):
    row, col = lax.axis_index("row"), lax.axis_index("col")
    copies[0].wait()
    used = (row == col) | (links[row, col] == 1)
    rows = buffer.shape[0] // LOADS
    for k in range(LOADS):
        copies[k + 1].wait()
        part = slice(k * rows, (k + 1) * rows)
        big_ref[:, part], small_ref[:, part] = split(jnp.where(used, buffer[part], 0.0).T)


def open_chain(factor_hbm, right_hbm, pattern_hbm, big_ref, small_ref, *rest):
    found, (right, buffer, links, sems) = rest[:PIECES], rest[PIECES:]
    count = found[0].shape[0]

    @pl.when(here(0, 0))
    def _():
        load = pltpu.make_async_copy(right_hbm, right, sems.at[LOADS + 1])
        load.start()
        copies = fetch(factor_hbm, pattern_hbm, buffer, links, sems)
        load.wait()
        rows = buffer.shape[0] // LOADS
        for k in range(LOADS):
            copies[k + 1].wait()
            part = slice(k * rows, (k + 1) * rows)
            answer = product(right[...], *split(buffer[part]), TURNED)
            for n, ref in enumerate(found):
                ref[:, part] = answer[n * count : (n + 1) * count]
        copies[0].wait()

    @pl.when(here(1, 0))
    def _():
        turn_block(fetch(factor_hbm, pattern_hbm, buffer, links, sems), buffer, links, big_ref, small_ref)

    @pl.when(jnp.logical_not(here(0, 0)))
    def _():
        for ref in found:
            ref[...] = jnp.zeros_like(ref)


def load_block(factor_hbm, right_hbm, pattern_hbm, *rest):
    big_ref, small_ref, *rest = rest[PIECES:]
    right, (buffer, links, sems) = rest[:PIECES], rest[PIECES:]
    count = right[0].shape[0]
    row, col = lax.axis_index("row"), lax.axis_index("col")

    @pl.when((row >= col) & jnp.logical_not(here(0, 0) | here(1, 0)))
    def _():
        loads = [
            pltpu.make_async_copy(right_hbm.at[pl.ds(n * count, count)], ref, sems.at[LOADS + 1 + n])
            for n, ref in enumerate(right)
        ]
        for load in loads:
            load.start()
        turn_block(fetch(factor_hbm, pattern_hbm, buffer, links, sems), buffer, links, big_ref, small_ref)
        for load in loads:
            load.wait()


def advance(rules, plain, big, small, held, *refs):
    sources, out = refs[:-1], refs[-1]
    out[...] = held[...]
    for spot in sorted({*rules, *plain}):

        @pl.when(here(*spot))
        def _(spot=spot):
            given = [source[...] for source in sources]
            terms = [product(rules[spot](*given), big[...], small[...], FLAT)] if spot in rules else []
            terms += [plain[spot](*given)] if spot in plain else []
            out[...] = sum(terms[1:], terms[0])


def share_of(ref, row):
    wide = ref.shape[1] // SIDE
    return ref[:, row * wide : (row + 1) * wide]


def step_one(big, small, held, right, second, out, side):
    out[...] = held[...]
    side[...] = jnp.zeros_like(side)

    @pl.when(here(1, 1))
    def _():
        out[...] = product(right[...] - second[...], big[...], small[...], FLAT)

    @pl.when(here(2, 0))
    def _():
        out[...] = second[...]
        side[...] = product(second[...], big[...], small[...], FLAT)


def join(held, side, out):
    out[...] = held[...]

    @pl.when(here(2, 1))
    def _():
        out[...] += side[...]


def pass_two(big, small, held, right, got, after, out):
    out[...] = held[...]

    @pl.when(here(2, 2))
    def _():
        out[...] = product(right[...] - got[...], big[...], small[...], FLAT)


def hand_over(*refs):
    solved, (across, zero, one) = refs[:PIECES], refs[PIECES:]
    count = solved[0].shape[0]
    row = lax.axis_index("row")
    for n, ref in enumerate(solved):
        part = slice(n * count, (n + 1) * count)
        for k in range(SIDE):

            @pl.when(row == (k ^ 1))
            def _(ref=ref, part=part, k=k):
                across[part] = share_of(ref, k)

        zero[part] = share_of(ref, 0)
        one[part] = share_of(ref, 1)


def hand_middle(*refs):
    held, inside, out = refs[:PIECES], refs[PIECES : 2 * PIECES], refs[-1]
    count = held[0].shape[0]
    for n in range(PIECES):
        part = slice(n * count, (n + 1) * count)
        out[part] = share_of(held[n], 0)

        @pl.when(here(3, 2))
        def _(n=n, part=part):
            out[part] = share_of(inside[n], 1)


def close_chain(piece, big, small, held, right, middle, got, out):
    out[...] = held[...]

    @pl.when(here(3, 3))
    def _():
        count = out.shape[0]
        columns = right[...] - middle[piece * count : (piece + 1) * count] - got[...]
        out[...] = product(columns, big[...], small[...], FLAT)


def beside_sum(big, small, *refs):
    beside, fourth, out = refs[:PIECES], refs[PIECES : 2 * PIECES], refs[-1]
    count = beside[0].shape[0]

    @pl.when(here(3, 1))
    def _():
        columns = jnp.concatenate([ref[...] for ref in beside], 0)
        answer = product(columns, big[...], small[...], FLAT)
        for n, ref in enumerate(fourth):
            part = slice(n * count, (n + 1) * count)
            out[part] = answer[part] + ref[...]

    @pl.when(jnp.logical_not(here(3, 1)))
    def _():
        out[...] = jnp.zeros_like(out)


def give(*refs):
    *lists, across, above, zero, one, out = refs
    count = out.shape[0] // PIECES
    share = {
        (0, 1): across, (2, 3): across,
        (0, 2): above, (1, 2): above, (0, 3): zero, (1, 3): one,
    }
    for (row, col), ref in share.items():

        @pl.when(here(row, col))
        def _(ref=ref):
            out[...] = ref[...]

    for n in range(PIECES):
        held, first, second, third, beside, inside = lists[n::PIECES]
        whole = {
            (0, 0): held, (1, 0): first, (2, 0): second, (3, 0): third,
            (1, 1): held, (2, 1): third, (3, 1): beside,
            (2, 2): held, (3, 2): inside, (3, 3): held,
        }
        for (row, col), ref in whole.items():

            @pl.when(here(row, col))
            def _(row=row, ref=ref, part=slice(n * count, (n + 1) * count)):
                out[part] = share_of(ref, row)


def route(*cycles):
    target = {}
    for cycle in cycles:
        for spot, source in enumerate(cycle):
            target[source] = cycle[(spot + 1) % len(cycle)]
    for row in range(SIDE):
        for col in range(SIDE):
            target.setdefault((row, col), (row ^ 1, col))
    assert sorted(target) == sorted(target.values())
    return [(a * SIDE + b, c * SIDE + d) for (a, b), (c, d) in target.items()]


ROUTES = {
    "solved_0": route(),
    "product_10": route([(1, 0), (1, 1), (0, 1), (0, 0), (2, 0), (3, 0)]),
    "solved_1": route([(1, 1), (2, 1), (3, 1), (0, 1)]),
    "product_20": route([(2, 0), (2, 1), (3, 1), (3, 0)]),
    "product_21": route([(2, 1), (2, 2), (3, 2), (1, 2), (0, 2), (2, 0), (3, 0), (3, 1)]),
    "beside": route(),
    "product_31": route([(3, 1), (3, 3), (2, 3), (2, 1)]),
    "solved_2": route(),
    "product_32": route([(3, 2), (3, 3), (2, 3), (2, 2)]),
    "share_2": route([(2, 2), (0, 2)], [(3, 2), (1, 2)]),
    "share_3": route(),
    "share_03": route([(3, 3), (0, 3), (1, 3), (2, 3)]),
    "share_13": route([(3, 3), (1, 3), (0, 3), (2, 3)]),
}


def send(name, array):
    with jax.named_scope(name):
        return lax.ppermute(array, GRID, ROUTES[name])


def chain(factor, rhs, pattern):
    block = factor[0, 0]
    order = block.shape[0]
    turned = rhs[0].T
    count = turned.shape[0] // PIECES
    half, vector = like(block, jnp.bfloat16), like(turned, shape=(count, order))
    work = 6 * order * order * count
    weight = dict(flops=work, size=4 * order * order)
    buffers = [pltpu.VMEM(block.shape, block.dtype), pltpu.SMEM(pattern.shape, pattern.dtype)]

    def move(name, rules, *lists, shared):
        return [
            call(functools.partial(advance, rules, {}), name, vector, (*shared, *args), **weight)
            for args in zip(*lists)
        ]

    def sends(name, arrays):
        return [send(name, array) for array in arrays]

    inputs = (block, turned, pattern)
    semaphores = pltpu.SemaphoreType.DMA((LOADS + 1 + PIECES,))
    big, small, *held = call(
        open_chain, "open_chain", [half, half] + [vector] * PIECES, inputs, [pltpu.HBM] * 3,
        [pltpu.VMEM(turned.shape, turned.dtype), *buffers, semaphores], **weight,
    )
    first = sends("solved_0", held)
    carried = move("product_10", {(1, 0): lambda first: first}, held, first, shared=(big, small))
    second = sends("product_10", carried)
    big, small, *right = call(
        load_block, "load_block", [half, half] + [vector] * PIECES, (*inputs, *carried), [pltpu.HBM] * 3 + [pltpu.VMEM] * PIECES,
        [*buffers, semaphores], **weight,
    )
    shared = (big, small)
    pairs = [
        call(step_one, "solve_1", [vector, vector], (*shared, *args), **weight) for args in zip(held, right, second)
    ]
    held, side = zip(*pairs)
    third, side = sends("solved_1", held), sends("product_20", side)
    carried = move("product_21", {(2, 1): lambda got: got, (3, 0): lambda got: got}, held, third, shared=shared)
    carried = [call(join, "join_2", vector, args, flops=1, size=1) for args in zip(carried, side)]
    fourth, beside = sends("product_21", carried), sends("beside", third)
    aside = call(beside_sum, "product_31", like(turned), (*shared, *beside, *fourth), **weight)
    middle = send("product_31", aside)
    after = fourth[0]
    solved, inside, last = [], [], []
    for n in range(PIECES):
        solved.append(call(pass_two, "solve_2", vector, (*shared, held[n], right[n], fourth[n], after), **weight))
        inside.append(send("solved_2", solved[n]))
        (after,) = move("product_32", {(3, 2): lambda got: got}, carried[n : n + 1], inside[n:], shared=shared)
        last.append(send("product_32", after))
    held = solved
    whole = like(turned, shape=(turned.shape[0], order // SIDE))
    above = send("share_2", call(hand_middle, "share_2", whole, (*held, *inside)))
    held = [
        call(functools.partial(close_chain, n), "solve_3", vector, (*shared, held[n], right[n], middle, last[n]), **weight)
        for n in range(PIECES)
    ]
    across, zero, one = call(hand_over, "share_3", [whole] * 3, held)
    across, zero, one = send("share_3", across), send("share_03", zero), send("share_13", one)
    lists = (held, first, second, third, beside, inside)
    given = call(give, "give", whole, [*[a for l in lists for a in l], across, above, zero, one])
    return given.T[None]


def from_root(shard, axis, root):
    mine = lax.axis_index(axis) == root
    return lax.psum(jnp.where(mine, shard, jnp.zeros_like(shard)), axis)


def multiply(factor_tile, columns):
    return jnp.dot(factor_tile, columns, precision=lax.Precision.HIGHEST, preferred_element_type=jnp.float32)


def levels(factor, rhs, pattern):
    block, right = factor[0, 0], rhs[0]
    row, col = lax.axis_index("row"), lax.axis_index("col")
    depth = min(6, lax.axis_size("row"))
    height = jnp.zeros((pattern.shape[0],), jnp.int32)
    for _ in range(depth):
        height = jnp.max(jnp.where(pattern == 1, height[None, :] + 1, 0), axis=1)
    solved = carried = jnp.zeros_like(right)
    times = functools.partial(multiply, block)
    for level in range(depth):
        solve_now = (row == col) & (height[row] == level)
        fresh = lax.cond(solve_now, times, jnp.zeros_like, right - carried)
        arrived = from_root(fresh, "row", col)
        if level < depth - 1:
            apply_now = (pattern[row, col] == 1) & (height[col] == level)
            carried = carried + lax.psum(lax.cond(apply_now, times, jnp.zeros_like, arrived), "col")
        solved = solved + arrived
    share = solved.shape[0] // lax.axis_size("row")
    return lax.dynamic_slice_in_dim(solved, row * share, share, 0)[None]


def solution(mesh):
    in_specs = (P(("grp", "row"), "col", None, None), P(("grp", "row"), None, None), P("grp", None))
    out_specs = P(("grp", "col"), "row", None)
    local = chain if mesh.shape["row"] == mesh.shape["col"] == SIDE else levels
    return jax.shard_map(local, mesh=mesh, in_specs=in_specs, out_specs=out_specs, check_vma=False)
```

```python
import functools

import jax
import jax.numpy as jnp
from jax import lax
from jax.experimental import pallas as pl
from jax.experimental.pallas import tpu as pltpu
from jax.sharding import PartitionSpec as P

GRID = ("row", "col")
LOADS = 3
PIECES = 2
FLAT = (((1,), (0,)), ((), ()))
TURNED = (((1,), (1,)), ((), ()))
SIDE = 4


def split(values):
    big = values.astype(jnp.bfloat16)
    return big, (values - big.astype(jnp.float32)).astype(jnp.bfloat16)


def product(columns, big, small, dims):
    count = columns.shape[0]
    high, low = split(columns)
    dot = functools.partial(lax.dot_general, dimension_numbers=dims, preferred_element_type=jnp.float32)
    both = dot(jnp.concatenate([high, low], 0), big)
    return both[:count] + (both[count:] + dot(high, small))


def here(row, col):
    return (lax.axis_index("row") == row) & (lax.axis_index("col") == col)


def call(kernel, name, outs, args, spaces=None, scratch=(), flops=0, size=0):
    spaces = spaces or [pltpu.VMEM] * len(args)
    many = isinstance(outs, list)
    kept = [pltpu.VMEM(out.shape, out.dtype) for out in (outs if many else [outs])]
    args = [pltpu.with_memory_space_constraint(a, s) if s is pltpu.HBM else a for a, s in zip(args, spaces)]
    found = pl.pallas_call(
        kernel,
        out_shape=kept,
        in_specs=[pl.BlockSpec(memory_space=space) for space in spaces],
        out_specs=[pl.BlockSpec(memory_space=pltpu.VMEM)] * len(kept),
        scratch_shapes=scratch,
        compiler_params=pltpu.CompilerParams(vmem_limit_bytes=24 << 20),
        cost_estimate=pl.CostEstimate(flops=flops, bytes_accessed=size, transcendentals=0),
        name=name,
    )(*args)
    return found if many else found[0]


def like(array, dtype=None, shape=None):
    return jax.ShapeDtypeStruct(shape or array.shape, dtype or array.dtype)


def fetch(factor_hbm, pattern_hbm, buffer, links, sems):
    rows = buffer.shape[0] // LOADS
    copies = [pltpu.make_async_copy(pattern_hbm, links, sems.at[LOADS])]
    for k in range(LOADS):
        part = pl.ds(k * rows, rows)
        copies.append(pltpu.make_async_copy(factor_hbm.at[part], buffer.at[part], sems.at[k]))
    for copy in copies:
        copy.start()
    return copies


def turn_block(copies, buffer, links, big_ref, small_ref):
    row, col = lax.axis_index("row"), lax.axis_index("col")
    copies[0].wait()
    used = (row == col) | (links[row, col] == 1)
    rows = buffer.shape[0] // LOADS
    for k in range(LOADS):
        copies[k + 1].wait()
        part = slice(k * rows, (k + 1) * rows)
        big_ref[:, part], small_ref[:, part] = split(jnp.where(used, buffer[part], 0.0).T)


def open_chain(factor_hbm, right_hbm, pattern_hbm, big_ref, small_ref, *rest):
    found, (right, buffer, links, sems) = rest[:PIECES], rest[PIECES:]
    count = found[0].shape[0]

    @pl.when(here(0, 0))
    def _():
        load = pltpu.make_async_copy(right_hbm, right, sems.at[LOADS + 1])
        load.start()
        copies = fetch(factor_hbm, pattern_hbm, buffer, links, sems)
        load.wait()
        rows = buffer.shape[0] // LOADS
        for k in range(LOADS):
            copies[k + 1].wait()
            part = slice(k * rows, (k + 1) * rows)
            answer = product(right[...], *split(buffer[part]), TURNED)
            for n, ref in enumerate(found):
                ref[:, part] = answer[n * count : (n + 1) * count]
        copies[0].wait()

    @pl.when(here(1, 0))
    def _():
        turn_block(fetch(factor_hbm, pattern_hbm, buffer, links, sems), buffer, links, big_ref, small_ref)

    @pl.when(jnp.logical_not(here(0, 0)))
    def _():
        for ref in found:
            ref[...] = jnp.zeros_like(ref)


def load_block(factor_hbm, right_hbm, pattern_hbm, *rest):
    big_ref, small_ref, *rest = rest[PIECES:]
    right, (buffer, links, sems) = rest[:PIECES], rest[PIECES:]
    count = right[0].shape[0]
    row, col = lax.axis_index("row"), lax.axis_index("col")

    @pl.when((row >= col) & jnp.logical_not(here(0, 0) | here(1, 0)))
    def _():
        loads = [
            pltpu.make_async_copy(right_hbm.at[pl.ds(n * count, count)], ref, sems.at[LOADS + 1 + n])
            for n, ref in enumerate(right)
        ]
        for load in loads:
            load.start()
        turn_block(fetch(factor_hbm, pattern_hbm, buffer, links, sems), buffer, links, big_ref, small_ref)
        for load in loads:
            load.wait()


def advance(rules, plain, big, small, held, *refs):
    sources, out = refs[:-1], refs[-1]
    out[...] = held[...]
    for spot in sorted({*rules, *plain}):

        @pl.when(here(*spot))
        def _(spot=spot):
            given = [source[...] for source in sources]
            terms = [product(rules[spot](*given), big[...], small[...], FLAT)] if spot in rules else []
            terms += [plain[spot](*given)] if spot in plain else []
            out[...] = sum(terms[1:], terms[0])


def share_of(ref, row):
    wide = ref.shape[1] // SIDE
    return ref[:, row * wide : (row + 1) * wide]


def step_one(big, small, held, right, second, out, side):
    out[...] = held[...]
    side[...] = jnp.zeros_like(side)

    @pl.when(here(1, 1))
    def _():
        out[...] = product(right[...] - second[...], big[...], small[...], FLAT)

    @pl.when(here(2, 0))
    def _():
        out[...] = second[...]
        side[...] = product(second[...], big[...], small[...], FLAT)


def join(held, side, out):
    out[...] = held[...]

    @pl.when(here(2, 1))
    def _():
        out[...] += side[...]


def pass_two(big, small, held, right, got, after, out):
    out[...] = held[...]

    @pl.when(here(2, 2))
    def _():
        out[...] = product(right[...] - got[...], big[...], small[...], FLAT)


def hand_over(*refs):
    solved, (zero, one) = refs[:PIECES], refs[PIECES:]
    count = solved[0].shape[0]
    for n, ref in enumerate(solved):
        part = slice(n * count, (n + 1) * count)
        zero[part] = share_of(ref, 0)
        one[part] = share_of(ref, 1)


def hand_across(*refs):
    solved, across = refs[:PIECES], refs[-1]
    count = solved[0].shape[0]
    row = lax.axis_index("row")
    for n, ref in enumerate(solved):
        part = slice(n * count, (n + 1) * count)
        for k in range(SIDE):

            @pl.when(row == (k ^ 1))
            def _(ref=ref, part=part, k=k):
                across[part] = share_of(ref, k)


def hand_middle(*refs):
    held, inside, out = refs[:PIECES], refs[PIECES : 2 * PIECES], refs[-1]
    count = held[0].shape[0]
    for n in range(PIECES):
        part = slice(n * count, (n + 1) * count)
        out[part] = share_of(held[n], 0)

        @pl.when(here(3, 2))
        def _(n=n, part=part):
            out[part] = share_of(inside[n], 1)


def close_chain(piece, big, small, held, right, middle, got, out):
    out[...] = held[...]

    @pl.when(here(3, 3))
    def _():
        count = out.shape[0]
        columns = right[...] - middle[piece * count : (piece + 1) * count] - got[...]
        out[...] = product(columns, big[...], small[...], FLAT)


def beside_sum(big, small, *refs):
    beside, fourth, out = refs[:PIECES], refs[PIECES : 2 * PIECES], refs[-1]
    count = beside[0].shape[0]

    @pl.when(here(3, 1))
    def _():
        columns = jnp.concatenate([ref[...] for ref in beside], 0)
        answer = product(columns, big[...], small[...], FLAT)
        for n, ref in enumerate(fourth):
            part = slice(n * count, (n + 1) * count)
            out[part] = answer[part] + ref[...]

    @pl.when(jnp.logical_not(here(3, 1)))
    def _():
        out[...] = jnp.zeros_like(out)


def give(*refs):
    *lists, across, above, zero, one, out = refs
    count = out.shape[0] // PIECES
    share = {
        (0, 1): across, (2, 3): across,
        (0, 2): above, (1, 2): above, (0, 3): zero, (1, 3): one,
    }
    for (row, col), ref in share.items():

        @pl.when(here(row, col))
        def _(ref=ref):
            out[...] = ref[...]

    for n in range(PIECES):
        held, first, second, third, beside, inside = lists[n::PIECES]
        whole = {
            (0, 0): held, (1, 0): first, (2, 0): second, (3, 0): third,
            (1, 1): held, (2, 1): third, (3, 1): beside,
            (2, 2): held, (3, 2): inside, (3, 3): held,
        }
        for (row, col), ref in whole.items():

            @pl.when(here(row, col))
            def _(row=row, ref=ref, part=slice(n * count, (n + 1) * count)):
                out[part] = share_of(ref, row)


def route(*cycles):
    target = {}
    for cycle in cycles:
        for spot, source in enumerate(cycle):
            target[source] = cycle[(spot + 1) % len(cycle)]
    for row in range(SIDE):
        for col in range(SIDE):
            target.setdefault((row, col), (row ^ 1, col))
    assert sorted(target) == sorted(target.values())
    return [(a * SIDE + b, c * SIDE + d) for (a, b), (c, d) in target.items()]


ROUTES = {
    "solved_0": route(),
    "product_10": route([(0, 0), (2, 0), (3, 0), (1, 3), (0, 3), (1, 0), (1, 1), (0, 1)]),
    "solved_1": route([(0, 1), (1, 1), (2, 1), (3, 1)]),
    "product_20": route([(2, 0), (2, 1), (3, 1), (3, 0)]),
    "product_21": route([(0, 2), (2, 0), (3, 0), (3, 1), (2, 1), (2, 2), (3, 2), (1, 2)]),
    "beside": route(),
    "product_31": route([(2, 1), (3, 1), (3, 3), (2, 3)]),
    "solved_2": route(),
    "product_32": route([(0, 2), (2, 2), (3, 2), (3, 3), (2, 3), (1, 3), (0, 3), (1, 2)]),
    "share_2": route([(0, 2), (2, 2)], [(1, 2), (3, 2)]),
    "share_3": route(),
    "share_03": route([(0, 3), (1, 3), (2, 3), (3, 3)]),
    "share_13": route([(0, 3), (2, 3), (3, 3), (1, 3)]),
}


def send(name, array):
    with jax.named_scope(name):
        return lax.ppermute(array, GRID, ROUTES[name])


def chain(factor, rhs, pattern):
    block = factor[0, 0]
    order = block.shape[0]
    turned = rhs[0].T
    count = turned.shape[0] // PIECES
    half, vector = like(block, jnp.bfloat16), like(turned, shape=(count, order))
    work = 6 * order * order * count
    weight = dict(flops=1, size=1)
    buffers = [pltpu.VMEM(block.shape, block.dtype), pltpu.SMEM(pattern.shape, pattern.dtype)]

    def move(name, rules, *lists, shared):
        return [
            call(functools.partial(advance, rules, {}), name, vector, (*shared, *args), **weight)
            for args in zip(*lists)
        ]

    def sends(name, arrays):
        return [send(name, array) for array in arrays]

    inputs = (block, turned, pattern)
    semaphores = pltpu.SemaphoreType.DMA((LOADS + 1 + PIECES,))
    big, small, *held = call(
        open_chain, "open_chain", [half, half] + [vector] * PIECES, inputs, [pltpu.HBM] * 3,
        [pltpu.VMEM(turned.shape, turned.dtype), *buffers, semaphores], **weight,
    )
    first = sends("solved_0", held)
    carried = move("product_10", {(1, 0): lambda first: first}, held, first, shared=(big, small))
    second = sends("product_10", carried)
    big, small, *right = call(
        load_block, "load_block", [half, half] + [vector] * PIECES, (*inputs, *carried), [pltpu.HBM] * 3 + [pltpu.VMEM] * PIECES,
        [*buffers, semaphores], **weight,
    )
    shared = (big, small)
    pairs = [
        call(step_one, "solve_1", [vector, vector], (*shared, *args), **weight) for args in zip(held, right, second)
    ]
    held, side = zip(*pairs)
    third, side = sends("solved_1", held), sends("product_20", side)
    carried = move("product_21", {(2, 1): lambda got: got, (3, 0): lambda got: got}, held, third, shared=shared)
    carried = [call(join, "join_2", vector, args, flops=1, size=1) for args in zip(carried, side)]
    fourth, beside = sends("product_21", carried), sends("beside", third)
    aside = call(beside_sum, "product_31", like(turned), (*shared, *beside, *fourth), **weight)
    middle = send("product_31", aside)
    after = fourth[0]
    solved, inside, last = [], [], []
    for n in range(PIECES):
        solved.append(call(pass_two, "solve_2", vector, (*shared, held[n], right[n], fourth[n], after), **weight))
        inside.append(send("solved_2", solved[n]))
        (after,) = move("product_32", {(3, 2): lambda got: got}, carried[n : n + 1], inside[n:], shared=shared)
        last.append(send("product_32", after))
    held = solved
    whole = like(turned, shape=(turned.shape[0], order // SIDE))
    above = send("share_2", call(hand_middle, "share_2", whole, (*held, *inside)))
    held = [
        call(functools.partial(close_chain, n), "solve_3", vector, (*shared, held[n], right[n], middle, last[n]), **weight)
        for n in range(PIECES)
    ]
    zero, one = call(hand_over, "share_3", [whole] * 2, held)
    across = call(hand_across, "across_3", whole, (*held, zero))
    across, zero, one = send("share_3", across), send("share_03", zero), send("share_13", one)
    lists = (held, first, second, third, beside, inside)
    given = call(give, "give", whole, [*[a for l in lists for a in l], across, above, zero, one])
    return given.T[None]


def from_root(shard, axis, root):
    mine = lax.axis_index(axis) == root
    return lax.psum(jnp.where(mine, shard, jnp.zeros_like(shard)), axis)


def multiply(factor_tile, columns):
    return jnp.dot(factor_tile, columns, precision=lax.Precision.HIGHEST, preferred_element_type=jnp.float32)


def levels(factor, rhs, pattern):
    block, right = factor[0, 0], rhs[0]
    row, col = lax.axis_index("row"), lax.axis_index("col")
    depth = min(6, lax.axis_size("row"))
    height = jnp.zeros((pattern.shape[0],), jnp.int32)
    for _ in range(depth):
        height = jnp.max(jnp.where(pattern == 1, height[None, :] + 1, 0), axis=1)
    solved = carried = jnp.zeros_like(right)
    times = functools.partial(multiply, block)
    for level in range(depth):
        solve_now = (row == col) & (height[row] == level)
        fresh = lax.cond(solve_now, times, jnp.zeros_like, right - carried)
        arrived = from_root(fresh, "row", col)
        if level < depth - 1:
            apply_now = (pattern[row, col] == 1) & (height[col] == level)
            carried = carried + lax.psum(lax.cond(apply_now, times, jnp.zeros_like, arrived), "col")
        solved = solved + arrived
    share = solved.shape[0] // lax.axis_size("row")
    return lax.dynamic_slice_in_dim(solved, row * share, share, 0)[None]


def solution(mesh):
    in_specs = (P(("grp", "row"), "col", None, None), P(("grp", "row"), None, None), P("grp", None))
    out_specs = P(("grp", "col"), "row", None)
    local = chain if mesh.shape["row"] == mesh.shape["col"] == SIDE else levels
    return jax.shard_map(local, mesh=mesh, in_specs=in_specs, out_specs=out_specs, check_vma=False)
```

```python
import functools

import jax
import jax.numpy as jnp
from jax import lax
from jax.experimental import pallas as pl
from jax.experimental.pallas import tpu as pltpu
from jax.sharding import PartitionSpec as P

GRID = ("row", "col")
LOADS = 2
PIECES = 2
FLAT = (((1,), (0,)), ((), ()))
TURNED = (((1,), (1,)), ((), ()))
SIDE = 4


def split(values):
    big = values.astype(jnp.bfloat16)
    return big, (values - big.astype(jnp.float32)).astype(jnp.bfloat16)


def product(columns, big, small, dims):
    count = columns.shape[0]
    high, low = split(columns)
    dot = functools.partial(lax.dot_general, dimension_numbers=dims, preferred_element_type=jnp.float32)
    both = dot(jnp.concatenate([high, low], 0), big)
    return both[:count] + (both[count:] + dot(high, small))


def here(row, col):
    return (lax.axis_index("row") == row) & (lax.axis_index("col") == col)


def call(kernel, name, outs, args, spaces=None, scratch=(), flops=0, size=0):
    spaces = spaces or [pltpu.VMEM] * len(args)
    many = isinstance(outs, list)
    kept = [pltpu.VMEM(out.shape, out.dtype) for out in (outs if many else [outs])]
    args = [pltpu.with_memory_space_constraint(a, s) if s is pltpu.HBM else a for a, s in zip(args, spaces)]
    found = pl.pallas_call(
        kernel,
        out_shape=kept,
        in_specs=[pl.BlockSpec(memory_space=space) for space in spaces],
        out_specs=[pl.BlockSpec(memory_space=pltpu.VMEM)] * len(kept),
        scratch_shapes=scratch,
        compiler_params=pltpu.CompilerParams(vmem_limit_bytes=24 << 20),
        cost_estimate=pl.CostEstimate(flops=flops, bytes_accessed=size, transcendentals=0),
        name=name,
    )(*args)
    return found if many else found[0]


def like(array, dtype=None, shape=None):
    return jax.ShapeDtypeStruct(shape or array.shape, dtype or array.dtype)


def fetch(factor_hbm, pattern_hbm, buffer, links, sems):
    rows = buffer.shape[0] // LOADS
    copies = [pltpu.make_async_copy(pattern_hbm, links, sems.at[LOADS])]
    for k in range(LOADS):
        part = pl.ds(k * rows, rows)
        copies.append(pltpu.make_async_copy(factor_hbm.at[part], buffer.at[part], sems.at[k]))
    for copy in copies:
        copy.start()
    return copies


def turn_block(copies, buffer, links, big_ref, small_ref):
    row, col = lax.axis_index("row"), lax.axis_index("col")
    copies[0].wait()
    used = (row == col) | (links[row, col] == 1)
    rows = buffer.shape[0] // LOADS
    for k in range(LOADS):
        copies[k + 1].wait()
        part = slice(k * rows, (k + 1) * rows)
        big_ref[:, part], small_ref[:, part] = split(jnp.where(used, buffer[part], 0.0).T)


def open_chain(factor_hbm, right_hbm, pattern_hbm, big_ref, small_ref, *rest):
    found, (right, buffer, links, sems) = rest[:PIECES], rest[PIECES:]
    count = found[0].shape[0]

    @pl.when(here(0, 0))
    def _():
        load = pltpu.make_async_copy(right_hbm, right, sems.at[LOADS + 1])
        load.start()
        copies = fetch(factor_hbm, pattern_hbm, buffer, links, sems)
        load.wait()
        rows = buffer.shape[0] // LOADS
        for k in range(LOADS):
            copies[k + 1].wait()
            part = slice(k * rows, (k + 1) * rows)
            answer = product(right[...], *split(buffer[part]), TURNED)
            for n, ref in enumerate(found):
                ref[:, part] = answer[n * count : (n + 1) * count]
        copies[0].wait()

    @pl.when(here(1, 0))
    def _():
        turn_block(fetch(factor_hbm, pattern_hbm, buffer, links, sems), buffer, links, big_ref, small_ref)

    @pl.when(jnp.logical_not(here(0, 0)))
    def _():
        for ref in found:
            ref[...] = jnp.zeros_like(ref)


def load_block(factor_hbm, right_hbm, pattern_hbm, *rest):
    big_ref, small_ref, *rest = rest[PIECES:]
    right, (buffer, links, sems) = rest[:PIECES], rest[PIECES:]
    count = right[0].shape[0]
    row, col = lax.axis_index("row"), lax.axis_index("col")

    @pl.when((row >= col) & jnp.logical_not(here(0, 0) | here(1, 0)))
    def _():
        loads = [
            pltpu.make_async_copy(right_hbm.at[pl.ds(n * count, count)], ref, sems.at[LOADS + 1 + n])
            for n, ref in enumerate(right)
        ]
        for load in loads:
            load.start()
        turn_block(fetch(factor_hbm, pattern_hbm, buffer, links, sems), buffer, links, big_ref, small_ref)
        for load in loads:
            load.wait()


def advance(rules, plain, big, small, held, *refs):
    sources, out = refs[:-1], refs[-1]
    out[...] = held[...]
    for spot in sorted({*rules, *plain}):

        @pl.when(here(*spot))
        def _(spot=spot):
            given = [source[...] for source in sources]
            terms = [product(rules[spot](*given), big[...], small[...], FLAT)] if spot in rules else []
            terms += [plain[spot](*given)] if spot in plain else []
            out[...] = sum(terms[1:], terms[0])


def share_of(ref, row):
    wide = ref.shape[1] // SIDE
    return ref[:, row * wide : (row + 1) * wide]


def step_one(big, small, held, right, second, out, side):
    out[...] = held[...]
    side[...] = jnp.zeros_like(side)

    @pl.when(here(1, 1))
    def _():
        out[...] = product(right[...] - second[...], big[...], small[...], FLAT)

    @pl.when(here(2, 0))
    def _():
        out[...] = second[...]
        side[...] = product(second[...], big[...], small[...], FLAT)


def join(held, side, out):
    out[...] = held[...]

    @pl.when(here(2, 1))
    def _():
        out[...] += side[...]


def pass_two(big, small, held, right, got, after, out):
    out[...] = held[...]

    @pl.when(here(2, 2))
    def _():
        out[...] = product(right[...] - got[...], big[...], small[...], FLAT)


def hand_over(*refs):
    solved, (zero, one) = refs[:PIECES], refs[PIECES:]
    count = solved[0].shape[0]
    for n, ref in enumerate(solved):
        part = slice(n * count, (n + 1) * count)
        zero[part] = share_of(ref, 0)
        one[part] = share_of(ref, 1)


def hand_across(*refs):
    solved, across = refs[:PIECES], refs[-1]
    count = solved[0].shape[0]
    row = lax.axis_index("row")
    for n, ref in enumerate(solved):
        part = slice(n * count, (n + 1) * count)
        for k in range(SIDE):

            @pl.when(row == (k ^ 1))
            def _(ref=ref, part=part, k=k):
                across[part] = share_of(ref, k)


def hand_middle(*refs):
    held, inside, out = refs[:PIECES], refs[PIECES : 2 * PIECES], refs[-1]
    count = held[0].shape[0]
    for n in range(PIECES):
        part = slice(n * count, (n + 1) * count)
        out[part] = share_of(held[n], 0)

        @pl.when(here(3, 2))
        def _(n=n, part=part):
            out[part] = share_of(inside[n], 1)


def close_chain(piece, big, small, held, right, middle, got, out):
    out[...] = held[...]

    @pl.when(here(3, 3))
    def _():
        count = out.shape[0]
        columns = right[...] - middle[piece * count : (piece + 1) * count] - got[...]
        out[...] = product(columns, big[...], small[...], FLAT)


def beside_sum(big, small, *refs):
    beside, fourth, out = refs[:PIECES], refs[PIECES : 2 * PIECES], refs[-1]
    count = beside[0].shape[0]

    @pl.when(here(3, 1))
    def _():
        columns = jnp.concatenate([ref[...] for ref in beside], 0)
        answer = product(columns, big[...], small[...], FLAT)
        for n, ref in enumerate(fourth):
            part = slice(n * count, (n + 1) * count)
            out[part] = answer[part] + ref[...]

    @pl.when(jnp.logical_not(here(3, 1)))
    def _():
        out[...] = jnp.zeros_like(out)


def give(*refs):
    *lists, across, above, zero, one, out = refs
    count = out.shape[0] // PIECES
    share = {
        (0, 1): across, (2, 3): across,
        (0, 2): above, (1, 2): above, (0, 3): zero, (1, 3): one,
    }
    for (row, col), ref in share.items():

        @pl.when(here(row, col))
        def _(ref=ref):
            out[...] = ref[...]

    for n in range(PIECES):
        held, first, second, third, beside, inside = lists[n::PIECES]
        whole = {
            (0, 0): held, (1, 0): first, (2, 0): second, (3, 0): third,
            (1, 1): held, (2, 1): third, (3, 1): beside,
            (2, 2): held, (3, 2): inside, (3, 3): held,
        }
        for (row, col), ref in whole.items():

            @pl.when(here(row, col))
            def _(row=row, ref=ref, part=slice(n * count, (n + 1) * count)):
                out[part] = share_of(ref, row)


def route(*cycles):
    target = {}
    for cycle in cycles:
        for spot, source in enumerate(cycle):
            target[source] = cycle[(spot + 1) % len(cycle)]
    for row in range(SIDE):
        for col in range(SIDE):
            target.setdefault((row, col), (row ^ 1, col))
    assert sorted(target) == sorted(target.values())
    return [(a * SIDE + b, c * SIDE + d) for (a, b), (c, d) in target.items()]


ROUTES = {
    "solved_0": route(),
    "product_10": route([(0, 0), (2, 0), (3, 0), (3, 2), (2, 2), (1, 0), (1, 1), (0, 1)]),
    "solved_1": route([(0, 1), (1, 1), (2, 1), (3, 1)]),
    "product_20": route([(2, 0), (2, 1), (3, 1), (3, 0)]),
    "product_21": route([(0, 2), (2, 0), (3, 0), (3, 1), (2, 1), (2, 2), (3, 2), (1, 2)]),
    "beside": route(),
    "product_31": route([(2, 1), (3, 1), (3, 3), (2, 3)]),
    "solved_2": route(),
    "product_32": route([(0, 2), (2, 2), (3, 2), (3, 3), (2, 3), (1, 3), (0, 3), (1, 2)]),
    "share_2": route([(0, 2), (2, 2)], [(1, 2), (3, 2)]),
    "share_3": route(),
    "share_03": route([(0, 3), (1, 3), (2, 3), (3, 3)]),
    "share_13": route([(0, 3), (2, 3), (3, 3), (1, 3)]),
}


def send(name, array):
    with jax.named_scope(name):
        return lax.ppermute(array, GRID, ROUTES[name])


def chain(factor, rhs, pattern):
    block = factor[0, 0]
    order = block.shape[0]
    turned = rhs[0].T
    count = turned.shape[0] // PIECES
    half, vector = like(block, jnp.bfloat16), like(turned, shape=(count, order))
    work = 6 * order * order * count
    weight = dict(flops=1, size=1)
    buffers = [pltpu.VMEM(block.shape, block.dtype), pltpu.SMEM(pattern.shape, pattern.dtype)]

    def move(name, rules, *lists, shared):
        return [
            call(functools.partial(advance, rules, {}), name, vector, (*shared, *args), **weight)
            for args in zip(*lists)
        ]

    def sends(name, arrays):
        return [send(name, array) for array in arrays]

    inputs = (block, turned, pattern)
    semaphores = pltpu.SemaphoreType.DMA((LOADS + 1 + PIECES,))
    big, small, *held = call(
        open_chain, "open_chain", [half, half] + [vector] * PIECES, inputs, [pltpu.HBM] * 3,
        [pltpu.VMEM(turned.shape, turned.dtype), *buffers, semaphores], **weight,
    )
    first = sends("solved_0", held)
    carried = move("product_10", {(1, 0): lambda first: first}, held, first, shared=(big, small))
    second = sends("product_10", carried)
    big, small, *right = call(
        load_block, "load_block", [half, half] + [vector] * PIECES, (*inputs, *carried), [pltpu.HBM] * 3 + [pltpu.VMEM] * PIECES,
        [*buffers, semaphores], **weight,
    )
    shared = (big, small)
    pairs = [
        call(step_one, "solve_1", [vector, vector], (*shared, *args), **weight) for args in zip(held, right, second)
    ]
    held, side = zip(*pairs)
    third, side = sends("solved_1", held), sends("product_20", side)
    carried = move("product_21", {(2, 1): lambda got: got, (3, 0): lambda got: got}, held, third, shared=shared)
    carried = [call(join, "join_2", vector, args, flops=1, size=1) for args in zip(carried, side)]
    fourth, beside = sends("product_21", carried), sends("beside", third)
    aside = call(beside_sum, "product_31", like(turned), (*shared, *beside, *fourth), **weight)
    middle = send("product_31", aside)
    after = fourth[0]
    solved, inside, last = [], [], []
    for n in range(PIECES):
        solved.append(call(pass_two, "solve_2", vector, (*shared, held[n], right[n], fourth[n], after), **weight))
        inside.append(send("solved_2", solved[n]))
        (after,) = move("product_32", {(3, 2): lambda got: got}, carried[n : n + 1], inside[n:], shared=shared)
        last.append(send("product_32", after))
    held = solved
    whole = like(turned, shape=(turned.shape[0], order // SIDE))
    above = send("share_2", call(hand_middle, "share_2", whole, (*held, *inside)))
    held = [
        call(functools.partial(close_chain, n), "solve_3", vector, (*shared, held[n], right[n], middle, last[n]), **weight)
        for n in range(PIECES)
    ]
    zero, one = call(hand_over, "share_3", [whole] * 2, held)
    across = call(hand_across, "across_3", whole, (*held, zero))
    across, zero, one = send("share_3", across), send("share_03", zero), send("share_13", one)
    lists = (held, first, second, third, beside, inside)
    given = call(give, "give", whole, [*[a for l in lists for a in l], across, above, zero, one])
    return given.T[None]


def from_root(shard, axis, root):
    mine = lax.axis_index(axis) == root
    return lax.psum(jnp.where(mine, shard, jnp.zeros_like(shard)), axis)


def multiply(factor_tile, columns):
    return jnp.dot(factor_tile, columns, precision=lax.Precision.HIGHEST, preferred_element_type=jnp.float32)


def levels(factor, rhs, pattern):
    block, right = factor[0, 0], rhs[0]
    row, col = lax.axis_index("row"), lax.axis_index("col")
    depth = min(6, lax.axis_size("row"))
    height = jnp.zeros((pattern.shape[0],), jnp.int32)
    for _ in range(depth):
        height = jnp.max(jnp.where(pattern == 1, height[None, :] + 1, 0), axis=1)
    solved = carried = jnp.zeros_like(right)
    times = functools.partial(multiply, block)
    for level in range(depth):
        solve_now = (row == col) & (height[row] == level)
        fresh = lax.cond(solve_now, times, jnp.zeros_like, right - carried)
        arrived = from_root(fresh, "row", col)
        if level < depth - 1:
            apply_now = (pattern[row, col] == 1) & (height[col] == level)
            carried = carried + lax.psum(lax.cond(apply_now, times, jnp.zeros_like, arrived), "col")
        solved = solved + arrived
    share = solved.shape[0] // lax.axis_size("row")
    return lax.dynamic_slice_in_dim(solved, row * share, share, 0)[None]


def solution(mesh):
    in_specs = (P(("grp", "row"), "col", None, None), P(("grp", "row"), None, None), P("grp", None))
    out_specs = P(("grp", "col"), "row", None)
    local = chain if mesh.shape["row"] == mesh.shape["col"] == SIDE else levels
    return jax.shard_map(local, mesh=mesh, in_specs=in_specs, out_specs=out_specs, check_vma=False)
```

```python
import functools

import jax
import jax.numpy as jnp
from jax import lax
from jax.experimental import pallas as pl
from jax.experimental.pallas import tpu as pltpu
from jax.sharding import PartitionSpec as P

GRID = ("row", "col")
LOADS = 2
PIECES = 2
FLAT = (((1,), (0,)), ((), ()))
TURNED = (((1,), (1,)), ((), ()))
SIDE = 4


def split(values):
    big = values.astype(jnp.bfloat16)
    return big, (values - big.astype(jnp.float32)).astype(jnp.bfloat16)


def product(columns, big, small, dims):
    count = columns.shape[0]
    high, low = split(columns)
    dot = functools.partial(lax.dot_general, dimension_numbers=dims, preferred_element_type=jnp.float32)
    both = dot(jnp.concatenate([high, low], 0), big)
    return both[:count] + (both[count:] + dot(high, small))


def here(row, col):
    return (lax.axis_index("row") == row) & (lax.axis_index("col") == col)


def call(kernel, name, outs, args, spaces=None, scratch=(), flops=0, size=0):
    spaces = spaces or [pltpu.VMEM] * len(args)
    many = isinstance(outs, list)
    kept = [pltpu.VMEM(out.shape, out.dtype) for out in (outs if many else [outs])]
    args = [pltpu.with_memory_space_constraint(a, s) if s is pltpu.HBM else a for a, s in zip(args, spaces)]
    found = pl.pallas_call(
        kernel,
        out_shape=kept,
        in_specs=[pl.BlockSpec(memory_space=space) for space in spaces],
        out_specs=[pl.BlockSpec(memory_space=pltpu.VMEM)] * len(kept),
        scratch_shapes=scratch,
        compiler_params=pltpu.CompilerParams(vmem_limit_bytes=24 << 20),
        cost_estimate=pl.CostEstimate(flops=flops, bytes_accessed=size, transcendentals=0),
        name=name,
    )(*args)
    return found if many else found[0]


def like(array, dtype=None, shape=None):
    return jax.ShapeDtypeStruct(shape or array.shape, dtype or array.dtype)


def fetch(factor_hbm, pattern_hbm, buffer, links, sems):
    rows = buffer.shape[0] // LOADS
    copies = [pltpu.make_async_copy(pattern_hbm, links, sems.at[LOADS])]
    for k in range(LOADS):
        part = pl.ds(k * rows, rows)
        copies.append(pltpu.make_async_copy(factor_hbm.at[part], buffer.at[part], sems.at[k]))
    for copy in copies:
        copy.start()
    return copies


def turn_block(copies, buffer, links, big_ref, small_ref):
    row, col = lax.axis_index("row"), lax.axis_index("col")
    copies[0].wait()
    used = (row == col) | (links[row, col] == 1)
    rows = buffer.shape[0] // LOADS
    for k in range(LOADS):
        copies[k + 1].wait()
        part = slice(k * rows, (k + 1) * rows)
        big_ref[:, part], small_ref[:, part] = split(jnp.where(used, buffer[part], 0.0).T)


def open_chain(factor_hbm, right_hbm, pattern_hbm, big_ref, small_ref, *rest):
    found, (right, buffer, links, sems) = rest[:PIECES], rest[PIECES:]
    count = found[0].shape[0]

    @pl.when(here(0, 0))
    def _():
        load = pltpu.make_async_copy(right_hbm, right, sems.at[LOADS + 1])
        load.start()
        copies = fetch(factor_hbm, pattern_hbm, buffer, links, sems)
        load.wait()
        rows = buffer.shape[0] // LOADS
        for k in range(LOADS):
            copies[k + 1].wait()
            part = slice(k * rows, (k + 1) * rows)
            answer = product(right[...], *split(buffer[part]), TURNED)
            for n, ref in enumerate(found):
                ref[:, part] = answer[n * count : (n + 1) * count]
        copies[0].wait()

    @pl.when(here(1, 0))
    def _():
        turn_block(fetch(factor_hbm, pattern_hbm, buffer, links, sems), buffer, links, big_ref, small_ref)

    @pl.when(jnp.logical_not(here(0, 0)))
    def _():
        for ref in found:
            ref[...] = jnp.zeros_like(ref)


def load_block(factor_hbm, right_hbm, pattern_hbm, *rest):
    big_ref, small_ref, *rest = rest[PIECES:]
    right, (buffer, links, sems) = rest[:PIECES], rest[PIECES:]
    count = right[0].shape[0]
    row, col = lax.axis_index("row"), lax.axis_index("col")

    @pl.when((row >= col) & jnp.logical_not(here(0, 0) | here(1, 0)))
    def _():
        loads = [
            pltpu.make_async_copy(right_hbm.at[pl.ds(n * count, count)], ref, sems.at[LOADS + 1 + n])
            for n, ref in enumerate(right)
        ]
        for load in loads:
            load.start()
        turn_block(fetch(factor_hbm, pattern_hbm, buffer, links, sems), buffer, links, big_ref, small_ref)
        for load in loads:
            load.wait()


def advance(rules, plain, big, small, held, *refs):
    sources, out = refs[:-1], refs[-1]
    out[...] = held[...]
    for spot in sorted({*rules, *plain}):

        @pl.when(here(*spot))
        def _(spot=spot):
            given = [source[...] for source in sources]
            terms = [product(rules[spot](*given), big[...], small[...], FLAT)] if spot in rules else []
            terms += [plain[spot](*given)] if spot in plain else []
            out[...] = sum(terms[1:], terms[0])


def share_of(ref, row):
    wide = ref.shape[1] // SIDE
    return ref[:, row * wide : (row + 1) * wide]


def step_one(big, small, held, right, second, out, side):
    out[...] = held[...]
    side[...] = jnp.zeros_like(side)

    @pl.when(here(1, 1))
    def _():
        out[...] = product(right[...] - second[...], big[...], small[...], FLAT)

    @pl.when(here(2, 0))
    def _():
        out[...] = second[...]
        side[...] = product(second[...], big[...], small[...], FLAT)


def join(held, side, out):
    out[...] = held[...]

    @pl.when(here(2, 1))
    def _():
        out[...] += side[...]


def pass_two(big, small, held, right, got, after, out):
    out[...] = held[...]

    @pl.when(here(2, 2))
    def _():
        out[...] = product(right[...] - got[...], big[...], small[...], FLAT)


def hand_over(*refs):
    solved, (zero, one) = refs[:PIECES], refs[PIECES:]
    count = solved[0].shape[0]
    for n, ref in enumerate(solved):
        part = slice(n * count, (n + 1) * count)
        zero[part] = share_of(ref, 0)
        one[part] = share_of(ref, 1)


def hand_across(*refs):
    solved, across = refs[:PIECES], refs[-1]
    count = solved[0].shape[0]
    row = lax.axis_index("row")
    for n, ref in enumerate(solved):
        part = slice(n * count, (n + 1) * count)
        for k in range(SIDE):

            @pl.when(row == (k ^ 1))
            def _(ref=ref, part=part, k=k):
                across[part] = share_of(ref, k)


def hand_middle(*refs):
    held, inside, out = refs[:PIECES], refs[PIECES : 2 * PIECES], refs[-1]
    count = held[0].shape[0]
    for n in range(PIECES):
        part = slice(n * count, (n + 1) * count)
        out[part] = share_of(held[n], 0)

        @pl.when(here(3, 2))
        def _(n=n, part=part):
            out[part] = share_of(inside[n], 1)


def close_chain(piece, big, small, held, right, middle, got, out):
    out[...] = held[...]

    @pl.when(here(3, 3))
    def _():
        count = out.shape[0]
        columns = right[...] - middle[piece * count : (piece + 1) * count] - got[...]
        out[...] = product(columns, big[...], small[...], FLAT)


def beside_sum(big, small, *refs):
    beside, fourth, out = refs[:PIECES], refs[PIECES : 2 * PIECES], refs[-1]
    count = beside[0].shape[0]

    @pl.when(here(3, 1))
    def _():
        columns = jnp.concatenate([ref[...] for ref in beside], 0)
        answer = product(columns, big[...], small[...], FLAT)
        for n, ref in enumerate(fourth):
            part = slice(n * count, (n + 1) * count)
            out[part] = answer[part] + ref[...]

    @pl.when(jnp.logical_not(here(3, 1)))
    def _():
        out[...] = jnp.zeros_like(out)


def give(*refs):
    *lists, across, above, zero, one, out = refs
    count = out.shape[0] // PIECES
    share = {
        (0, 1): across, (2, 3): across,
        (0, 2): above, (1, 2): above, (0, 3): zero, (1, 3): one,
    }
    for (row, col), ref in share.items():

        @pl.when(here(row, col))
        def _(ref=ref):
            out[...] = ref[...]

    for n in range(PIECES):
        held, first, second, third, beside, inside = lists[n::PIECES]
        whole = {
            (0, 0): held, (1, 0): first, (2, 0): second, (3, 0): third,
            (1, 1): held, (2, 1): third, (3, 1): beside,
            (2, 2): held, (3, 2): inside, (3, 3): held,
        }
        for (row, col), ref in whole.items():

            @pl.when(here(row, col))
            def _(row=row, ref=ref, part=slice(n * count, (n + 1) * count)):
                out[part] = share_of(ref, row)


def route(*cycles):
    target = {}
    for cycle in cycles:
        for spot, source in enumerate(cycle):
            target[source] = cycle[(spot + 1) % len(cycle)]
    for row in range(SIDE):
        for col in range(SIDE):
            target.setdefault((row, col), (row ^ 1, col))
    assert sorted(target) == sorted(target.values())
    return [(a * SIDE + b, c * SIDE + d) for (a, b), (c, d) in target.items()]


ROUTES = {
    "solved_0": route(),
    "product_10": route([(0, 0), (2, 0), (3, 0), (3, 2), (2, 2), (1, 0), (1, 1), (0, 1)]),
    "solved_1": route([(0, 1), (1, 1), (2, 1), (3, 1)]),
    "product_20": route([(2, 0), (2, 1), (3, 1), (3, 0)]),
    "product_21": route([(0, 2), (2, 0), (3, 0), (3, 1), (2, 1), (2, 2), (3, 2), (1, 2)]),
    "beside": route(),
    "product_31": route([(2, 1), (3, 1), (3, 3), (2, 3)]),
    "solved_2": route(),
    "product_32": route([(0, 2), (2, 2), (3, 2), (3, 3), (2, 3), (1, 3), (0, 3), (1, 2)]),
    "share_2": [(2 * SIDE + 2, 2), (3 * SIDE + 2, SIDE + 2)],
    "share_3": route(),
    "share_03": route([(0, 3), (1, 3), (2, 3), (3, 3)]),
    "share_13": route([(0, 3), (2, 3), (3, 3), (1, 3)]),
}


def send(name, array):
    with jax.named_scope(name):
        return lax.ppermute(array, GRID, ROUTES[name])


def chain(factor, rhs, pattern):
    block = factor[0, 0]
    order = block.shape[0]
    turned = rhs[0].T
    count = turned.shape[0] // PIECES
    half, vector = like(block, jnp.bfloat16), like(turned, shape=(count, order))
    work = 6 * order * order * count
    weight = dict(flops=1, size=1)
    buffers = [pltpu.VMEM(block.shape, block.dtype), pltpu.SMEM(pattern.shape, pattern.dtype)]

    def move(name, rules, *lists, shared):
        return [
            call(functools.partial(advance, rules, {}), name, vector, (*shared, *args), **weight)
            for args in zip(*lists)
        ]

    def sends(name, arrays):
        return [send(name, array) for array in arrays]

    inputs = (block, turned, pattern)
    semaphores = pltpu.SemaphoreType.DMA((LOADS + 1 + PIECES,))
    big, small, *held = call(
        open_chain, "open_chain", [half, half] + [vector] * PIECES, inputs, [pltpu.HBM] * 3,
        [pltpu.VMEM(turned.shape, turned.dtype), *buffers, semaphores], **weight,
    )
    first = sends("solved_0", held)
    carried = move("product_10", {(1, 0): lambda first: first}, held, first, shared=(big, small))
    second = sends("product_10", carried)
    big, small, *right = call(
        load_block, "load_block", [half, half] + [vector] * PIECES, (*inputs, *carried), [pltpu.HBM] * 3 + [pltpu.VMEM] * PIECES,
        [*buffers, semaphores], **weight,
    )
    shared = (big, small)
    pairs = [
        call(step_one, "solve_1", [vector, vector], (*shared, *args), **weight) for args in zip(held, right, second)
    ]
    held, side = zip(*pairs)
    third, side = sends("solved_1", held), sends("product_20", side)
    carried = move("product_21", {(2, 1): lambda got: got, (3, 0): lambda got: got}, held, third, shared=shared)
    carried = [call(join, "join_2", vector, args, flops=1, size=1) for args in zip(carried, side)]
    fourth, beside = sends("product_21", carried), sends("beside", third)
    aside = call(beside_sum, "product_31", like(turned), (*shared, *beside, *fourth), **weight)
    middle = send("product_31", aside)
    after = fourth[0]
    solved, inside, last = [], [], []
    for n in range(PIECES):
        solved.append(call(pass_two, "solve_2", vector, (*shared, held[n], right[n], fourth[n], after), **weight))
        inside.append(send("solved_2", solved[n]))
        (after,) = move("product_32", {(3, 2): lambda got: got}, carried[n : n + 1], inside[n:], shared=shared)
        last.append(send("product_32", after))
    held = solved
    whole = like(turned, shape=(turned.shape[0], order // SIDE))
    above = send("share_2", call(hand_middle, "share_2", whole, (*held, *inside)))
    held = [
        call(functools.partial(close_chain, n), "solve_3", vector, (*shared, held[n], right[n], middle, last[n]), **weight)
        for n in range(PIECES)
    ]
    zero, one = call(hand_over, "share_3", [whole] * 2, held)
    across = call(hand_across, "across_3", whole, (*held, zero))
    across, zero, one = send("share_3", across), send("share_03", zero), send("share_13", one)
    lists = (held, first, second, third, beside, inside)
    given = call(give, "give", whole, [*[a for l in lists for a in l], across, above, zero, one])
    return given.T[None]


def from_root(shard, axis, root):
    mine = lax.axis_index(axis) == root
    return lax.psum(jnp.where(mine, shard, jnp.zeros_like(shard)), axis)


def multiply(factor_tile, columns):
    return jnp.dot(factor_tile, columns, precision=lax.Precision.HIGHEST, preferred_element_type=jnp.float32)


def levels(factor, rhs, pattern):
    block, right = factor[0, 0], rhs[0]
    row, col = lax.axis_index("row"), lax.axis_index("col")
    depth = min(6, lax.axis_size("row"))
    height = jnp.zeros((pattern.shape[0],), jnp.int32)
    for _ in range(depth):
        height = jnp.max(jnp.where(pattern == 1, height[None, :] + 1, 0), axis=1)
    solved = carried = jnp.zeros_like(right)
    times = functools.partial(multiply, block)
    for level in range(depth):
        solve_now = (row == col) & (height[row] == level)
        fresh = lax.cond(solve_now, times, jnp.zeros_like, right - carried)
        arrived = from_root(fresh, "row", col)
        if level < depth - 1:
            apply_now = (pattern[row, col] == 1) & (height[col] == level)
            carried = carried + lax.psum(lax.cond(apply_now, times, jnp.zeros_like, arrived), "col")
        solved = solved + arrived
    share = solved.shape[0] // lax.axis_size("row")
    return lax.dynamic_slice_in_dim(solved, row * share, share, 0)[None]


def solution(mesh):
    in_specs = (P(("grp", "row"), "col", None, None), P(("grp", "row"), None, None), P("grp", None))
    out_specs = P(("grp", "col"), "row", None)
    local = chain if mesh.shape["row"] == mesh.shape["col"] == SIDE else levels
    return jax.shard_map(local, mesh=mesh, in_specs=in_specs, out_specs=out_specs, check_vma=False)
```
